32 devices in a mesh: seq: 32 (over z, y, x, core).
Axes of the slice: x: 2, y: 2, z: 4, core: 2. Of those that a mesh axis runs over, the one named last changes fastest.
Arguments:
- queries: bfloat16 [16384, 384], P('seq'), may hold values from -12 to 12
- keys: bfloat16 [16384, 384], P('seq'), may hold values from -6 to 6
- values: bfloat16 [16384, 384], P('seq'), may hold values from -6 to 6
- out_weight: bfloat16 [384, 768], replicated, may hold values from -0.3125 to 0.3125
Outputs:
- layer_out: bfloat16 [16384, 768], P('seq')
The draws below stay inside these ranges and needn't reach their ends.
All inputs are finite; a program needn't handle non-finite values.
Results may differ from the reference program's by a relative error of at most 0.0054.
Values may be sent and summed in bfloat16 or wider, within the bound.
A program may use at most 128 MiB of HBM per device.

```python
import math
import jax
import jax.numpy as jnp
from jax import lax

D = 768
HEAD_COUNT = 6
HEAD_SIZE = 64
DEVICE_TOKENS = 512
FIRST_DILATION = 8
SECOND_DILATION = 32
THIRD_DILATION = 128
ATT = 384
FIRST_GROUP = 2
SECOND_GROUP = 8
SEQUENCE_TOKENS = 16384


def draw_queries(key, part):
    key = jax.random.fold_in(key, 7)
    width = HEAD_COUNT * HEAD_SIZE
    base = jnp.clip(1.5 * jax.random.normal(key, (SEQUENCE_TOKENS, width), jnp.float32), -9.0, 9.0)
    return base.astype(jnp.bfloat16)


def draw_keys(key, part):
    key = jax.random.fold_in(key, 11)
    width = HEAD_COUNT * HEAD_SIZE
    base = jnp.clip(jax.random.normal(key, (SEQUENCE_TOKENS, width), jnp.float32), -6.0, 6.0)
    return base.astype(jnp.bfloat16)


def steps_of(stream_key, extent, shards, least, top_value):
    def one(position, blocks):
        steps = jax.random.uniform(jax.random.fold_in(jax.random.fold_in(stream_key, 6), position), (blocks,), jnp.float32, least / len(shards), top_value / len(shards))
        return jnp.repeat(jnp.exp(steps), extent[position] // blocks).reshape((-1,) + (1,) * (len(extent) - position - 1))

    loudness = one(*shards[0])
    for cut in shards[1:]:
        loudness = loudness * one(*cut)
    return loudness


def normal_values(key, extent, spread, bound, cuts=(), held_as=jnp.bfloat16):
    loudness = steps_of(key, extent, cuts, -0.22, 0.18) if cuts else 1.0
    entries = jax.random.normal(key, extent, jnp.float32) * spread * loudness
    return jnp.minimum(jnp.maximum(entries, -bound), bound).astype(held_as)


def setup_inputs(seed: int = 0) -> dict:
    key_list = jax.random.split(jax.random.key(seed), 5)
    return {
        "queries": draw_queries(jax.random.fold_in(key_list[4], 71), 0),
        "keys": draw_keys(jax.random.fold_in(key_list[4], 71), 0),
        "values": normal_values(key_list[2], (SEQUENCE_TOKENS, ATT), 1.0, 6.0, ((0, 32),)),
        "out_weight": normal_values(key_list[3], (ATT, D), ATT ** -0.5, 0.3125),
    }


def attend(query, keyval):
    rows = keyval.shape[0]
    heads = query.shape[1]
    size = query.shape[2]
    width = heads * size
    key_part = keyval[:, :width].reshape(rows, heads, size).astype(jnp.float32)
    value_part = keyval[:, width:].reshape(rows, heads, size).astype(jnp.float32)
    scores = jnp.einsum('qhd,khd->hqk', query.astype(jnp.float32), key_part) / math.sqrt(size)
    top = lax.optimization_barrier(jnp.max(scores, axis=2, keepdims=True))
    prob = jnp.exp(scores - top)
    total = lax.optimization_barrier(jnp.sum(prob, axis=2))
    weights = lax.optimization_barrier(prob.astype(jnp.bfloat16))
    attended = jnp.einsum('hqk,khd->qhd', weights.astype(jnp.float32), value_part) / total.T[:, :, None]
    log_total = (top[:, :, 0] + jnp.log(total)).T
    return (attended, log_total)

def pick_rows(matrix, dilation):
    token_index = jnp.arange(HEAD_COUNT)
    shaped = matrix.reshape(matrix.shape[0] // dilation, dilation, HEAD_COUNT, HEAD_SIZE)
    return shaped[:, token_index % dilation, token_index]

def merge_pair(first_out, first_lse, second_out, second_lse):
    larger = jnp.maximum(first_lse, second_lse)
    first_w = jnp.exp(first_lse - larger)
    second_w = jnp.exp(second_lse - larger)
    summed = first_w + second_w
    merged = (first_w[..., None] * first_out + second_w[..., None] * second_out) / summed[..., None]
    return (merged, larger + jnp.log(summed))

def fold_broad_level(narrow_output, narrow_log_sum, broad_output, broad_log_sum, dilation_ratio, narrow_dilation):
    token_index = jnp.arange(HEAD_COUNT)
    segment_places = token_index // narrow_dilation
    reshaped_output = narrow_output.reshape(-1, dilation_ratio, HEAD_COUNT, HEAD_SIZE)
    reshaped_log_sum = narrow_log_sum.reshape(-1, dilation_ratio, HEAD_COUNT)
    merged, merged_lse = merge_pair(reshaped_output[:, segment_places, token_index], reshaped_log_sum[:, segment_places, token_index], broad_output, broad_log_sum)
    reshaped_output = reshaped_output.at[:, segment_places, token_index].set(merged)
    reshaped_log_sum = reshaped_log_sum.at[:, segment_places, token_index].set(merged_lse)
    return (reshaped_output.reshape(narrow_output.shape), reshaped_log_sum.reshape(narrow_log_sum.shape))

def dilated_level(queries, keys, values, dilation, segment):
    width = HEAD_COUNT * HEAD_SIZE
    picked_q = pick_rows(queries, dilation)
    count = picked_q.shape[0]
    picked_kv = jnp.concatenate([pick_rows(keys, dilation).reshape(count, width), pick_rows(values, dilation).reshape(count, width)], axis=1)
    per_seg = segment // dilation
    seg_q = picked_q.reshape(count // per_seg, per_seg, HEAD_COUNT, HEAD_SIZE)
    seg_kv = picked_kv.reshape(count // per_seg, per_seg, 2 * width)
    result, lse = lax.map(lambda pair: attend(pair[0], pair[1]), (seg_q, seg_kv))
    return (result.reshape(count, HEAD_COUNT, HEAD_SIZE), lse.reshape(count, HEAD_COUNT))

def reference(queries, keys, values, out_weight):
    width = HEAD_COUNT * HEAD_SIZE
    output_third, log_sum_third = dilated_level(queries, keys, values, THIRD_DILATION, SEQUENCE_TOKENS)
    output_second, log_sum_second = dilated_level(queries, keys, values, SECOND_DILATION, SECOND_GROUP * DEVICE_TOKENS)
    output_first, log_sum_first = dilated_level(queries, keys, values, FIRST_DILATION, FIRST_GROUP * DEVICE_TOKENS)
    output_second, log_sum_second = fold_broad_level(output_second, log_sum_second, output_third, log_sum_third, THIRD_DILATION // SECOND_DILATION, SECOND_DILATION)
    output_first, log_sum_first = fold_broad_level(output_first, log_sum_first, output_second, log_sum_second, SECOND_DILATION // FIRST_DILATION, FIRST_DILATION)
    blocks = SEQUENCE_TOKENS // DEVICE_TOKENS
    block_q = queries.reshape(blocks, DEVICE_TOKENS, HEAD_COUNT, HEAD_SIZE)
    block_kv = jnp.concatenate([keys, values], axis=1).reshape(blocks, DEVICE_TOKENS, 2 * width)
    block_output, block_log_sum = lax.map(lambda pair: attend(pair[0], pair[1]), (block_q, block_kv))
    token_index = jnp.arange(HEAD_COUNT)
    segment_places = token_index % FIRST_DILATION
    reshaped_output = block_output.reshape(SEQUENCE_TOKENS // FIRST_DILATION, FIRST_DILATION, HEAD_COUNT, HEAD_SIZE)
    reshaped_log_sum = block_log_sum.reshape(SEQUENCE_TOKENS // FIRST_DILATION, FIRST_DILATION, HEAD_COUNT)
    merged, merged_lse = merge_pair(reshaped_output[:, segment_places, token_index], reshaped_log_sum[:, segment_places, token_index], output_first, log_sum_first)
    reshaped_output = reshaped_output.at[:, segment_places, token_index].set(merged)
    combined = reshaped_output.reshape(SEQUENCE_TOKENS, width).astype(jnp.bfloat16)
    return jnp.dot(combined, out_weight, preferred_element_type=jnp.float32).astype(jnp.bfloat16)
```

```python
import functools
import math

import jax
import jax.numpy as jnp
from jax import lax
from jax.experimental import pallas as pl
from jax.experimental.pallas import tpu as pltpu
from jax.sharding import PartitionSpec as P

HEAD_COUNT = 6
HEAD_SIZE = 64
PAIRS = HEAD_COUNT // 2
FIRST_DILATION = 8
WIDTH = HEAD_COUNT * HEAD_SIZE
LANES = 2 * HEAD_SIZE
ABSENT = -1e30
SCALE = math.log2(math.e) / math.sqrt(HEAD_SIZE)
MESH = pl.DeviceIdType.MESH
QUERY_CHUNK = 256


def iota(shape, axis):
    return lax.broadcasted_iota(jnp.int32, shape, axis)


def one_hot_rows(pair, tokens):
    row = iota((LANES, 1), 0)
    half = row >> 6
    slot = row & 63
    turned = (slot - 4 * pair) & 15
    rest = turned - 4
    third = rest * 43 >> 7
    second_place = jnp.where(turned < 4, 16 * turned, 16 * third + 4 * (rest - 3 * third + 1))
    other = slot - 16
    third = other * 43 >> 7
    first_place = 4 * third + (other - 3 * third) + 1
    place = jnp.where(slot < 16, second_place, first_place)
    token = FIRST_DILATION * place + 2 * pair + half
    return jnp.where(iota((LANES, tokens), 1) == token, 1.0, 0.0).astype(jnp.bfloat16)


def dot(a, b, dims=((1,), (0,))):
    return lax.dot_general(a, b, (dims, ((), ())), preferred_element_type=jnp.float32)


def partial_softmax(scores, value, value_dim):
    top = jnp.max(scores, axis=0, keepdims=True)
    prob = jnp.exp2((scores - top) * SCALE)
    total = jnp.sum(prob, axis=0, keepdims=True)
    return top, total, dot(value, prob.astype(jnp.bfloat16), ((value_dim,), (0,)))


def join(parts):
    top = functools.reduce(jnp.maximum, [p[0] for p in parts])
    weights = [jnp.exp2((p[0] - top) * SCALE) for p in parts]
    total = sum(w * p[1] for w, p in zip(weights, parts))
    return sum(w * p[2] for w, p in zip(weights, parts)) * (1.0 / total)


def kernel(
    chips, q_hbm, k_hbm, v_hbm, w_hbm, out_hbm,
    q_ref, k_ref, v_ref, w_ref, out_ref, comb, spread, vt, qbd, near, middle, whole,
    in_sem, out_sem, send_sem, recv_sem, mate_send, mate_recv,
):
    tokens = q_ref.shape[0]
    me = lax.axis_index("seq")
    chip = lax.div(me, 2)
    core = lax.rem(me, 2)
    mate = chip * 2 + 1 - core
    bufs = (near, middle, whole)

    loads = []
    for n, (src, dst) in enumerate(((k_hbm, k_ref), (v_hbm, v_ref), (q_hbm, q_ref), (w_hbm, w_ref))):
        loads.append(pltpu.make_async_copy(src, dst, in_sem.at[n]))
        loads[-1].start()

    barrier = pltpu.get_barrier_semaphore()
    pl.semaphore_signal(barrier, inc=1, device_id=(mate,), device_id_type=MESH)

    def over(count, body):
        if count <= 16:
            for d in range(1, count):
                body(d)
        else:
            lax.fori_loop(1, count, lambda d, _: (body(d), 0)[1], 0)

    def peer(count, d):
        place = lax.rem(chip, count)
        return (chip - place + lax.rem(place + d, count)) * 2 + core

    total_chips = chips[2]

    def greet(d):
        pl.semaphore_signal(
            barrier, inc=1, device_id=(peer(total_chips, d),), device_id_type=MESH
        )

    over(total_chips, greet)

    block_diagonal = (iota((LANES, LANES), 0) >> 6) == (iota((LANES, LANES), 1) >> 6)
    for t in range(PAIRS):
        spread[t] = one_hot_rows(t, tokens)

    places = [lax.rem(chip, c) for c in chips]
    slot_pair = iota((16, LANES), 0) >> 2
    for n, src in enumerate((k_ref, v_ref)):
        loads[n].wait()
        packed = jnp.zeros((16, LANES), jnp.float32)
        for t in range(PAIRS):
            picked = dot(spread[t], src[:, t * LANES:(t + 1) * LANES])
            picked = jnp.where(block_diagonal, picked, 0.0)
            rows = picked[:HEAD_SIZE] + picked[HEAD_SIZE:]
            packed = jnp.where(slot_pair == t, rows[:16], packed)
            rows = rows.astype(jnp.bfloat16)
            first = n * WIDTH + t * LANES
            near[core, places[0], :, first:first + LANES] = rows
            middle[core, places[1], :, first:first + LANES] = rows[:16]
        whole[core, places[2], :, n * LANES:(n + 1) * LANES] = packed.astype(jnp.bfloat16)

    pl.semaphore_wait(barrier, total_chips)

    for level in (2, 1, 0):
        own = bufs[level].at[core, places[level]]

        def send(d, level=level, own=own):
            pltpu.make_async_remote_copy(
                src_ref=own,
                dst_ref=own,
                send_sem=send_sem.at[level],
                recv_sem=recv_sem.at[level],
                device_id=(peer(chips[level], d),),
                device_id_type=MESH,
            ).start()

        over(chips[level], send)

    def to_mate(level):
        part = bufs[level].at[core]
        return pltpu.make_async_remote_copy(
            src_ref=part,
            dst_ref=part,
            send_sem=mate_send.at[level],
            recv_sem=mate_recv.at[level],
            device_id=(mate,),
            device_id_type=MESH,
        )

    def others(level, sem):
        part = bufs[level].at[core, pl.ds(0, chips[level] - 1)]
        return pltpu.make_async_copy(part, part, sem.at[level])

    def forward(level):
        if chips[level] > 1:
            others(level, recv_sem).wait()
        to_mate(level).start()

    if chips[0] == 1:
        forward(0)

    vt[...] = v_ref[...].T
    loads[2].wait()
    for t in range(PAIRS):
        picked = dot(spread[t], q_ref[:, t * LANES:(t + 1) * LANES])
        qbd[t] = jnp.where(block_diagonal, picked, 0.0).astype(jnp.bfloat16)

    lane_half = iota((QUERY_CHUNK, LANES), 1) >> 6

    def local_heads(heads):
        for h in heads:
            t, e = divmod(h, 2)
            key = k_ref[:, t * LANES:(t + 1) * LANES]
            value = vt[h * HEAD_SIZE:(h + 1) * HEAD_SIZE]
            for first in range(0, tokens, QUERY_CHUNK):
                query = q_ref[first:first + QUERY_CHUNK, t * LANES:(t + 1) * LANES]
                query = jnp.where(lane_half == e, query, jnp.zeros_like(query))
                _, total, out = partial_softmax(dot(key, query, ((1,), (1,))), value, 1)
                comb[h * HEAD_SIZE:(h + 1) * HEAD_SIZE, first:first + QUERY_CHUNK] = (
                    out * (1.0 / total)
                ).astype(jnp.bfloat16)

    local_heads(range(0, 3))
    for level in (1, 2) if chips[0] == 1 else (0, 1, 2):
        forward(level)
    local_heads(range(3, HEAD_COUNT))

    parts = []
    for t in range(PAIRS):
        columns = slice(t * LANES, (t + 1) * LANES)
        scores = dot(k_ref[:, columns], qbd[t], ((1,), (1,)))
        parts.append([partial_softmax(scores, vt[columns], 1)])

    for level in range(3):
        to_mate(level).wait()

    def rows_of(buf, first):
        block = buf[:, :, :, first:first + LANES]
        return block.reshape(-1, LANES)

    lane_slot = iota((1, LANES), 1) & 63
    slot_rows = (iota((LANES, LANES), 0) & 63) >> 2
    query = jnp.zeros((LANES, LANES), jnp.float32)
    for t in range(PAIRS):
        query = jnp.where(slot_rows == t, qbd[t].astype(jnp.float32), query)
    scores = dot(rows_of(whole, 0), query.astype(jnp.bfloat16), ((1,), (1,)))
    row_pair = (iota(scores.shape, 0) & 15) >> 2
    scores = jnp.where(row_pair == (lane_slot >> 2), scores, ABSENT)
    top3, total3, out3 = partial_softmax(scores, rows_of(whole, LANES), 0)

    for t in range(PAIRS):
        columns = slice(t * LANES, (t + 1) * LANES)
        scores = dot(rows_of(near, t * LANES), qbd[t], ((1,), (1,)))
        parts[t].append(partial_softmax(scores, rows_of(near, WIDTH + t * LANES), 0))
        scores = dot(rows_of(middle, t * LANES), qbd[t], ((1,), (1,)))
        top, total, out = partial_softmax(scores, rows_of(middle, WIDTH + t * LANES), 0)
        parts[t].append((jnp.where(lane_slot < 16, top, ABSENT), total, out))
        parts[t].append((jnp.where((lane_slot >> 2) == t, top3, ABSENT), total3, out3))
        merged = jnp.where(block_diagonal, join(parts[t]), 0.0).astype(jnp.bfloat16)
        placed = dot(merged, spread[t])
        head = 2 * t + (iota(placed.shape, 0) >> 6)
        chosen = (iota(placed.shape, 1) & (FIRST_DILATION - 1)) == head
        comb[columns] = jnp.where(
            chosen, placed, comb[columns].astype(jnp.float32)
        ).astype(jnp.bfloat16)

    loads[3].wait()
    stores = []
    for n, first in enumerate(range(0, tokens, QUERY_CHUNK)):
        rows = slice(first, first + QUERY_CHUNK)
        out_ref[rows] = dot(comb[:, rows].T, w_ref[...]).astype(jnp.bfloat16)
        stores.append(pltpu.make_async_copy(out_ref.at[rows], out_hbm.at[rows], out_sem.at[n]))
        stores[-1].start()

    for level in range(3):
        if chips[level] > 1:
            others(level, send_sem).wait()
    for store in stores:
        store.wait()


def on_device(queries, keys, values, out_weight):
    devices = lax.axis_size("seq")
    tokens = queries.shape[0]
    columns = out_weight.shape[1]
    chips = (devices // 32, devices // 8, devices // 2)
    bf16 = jnp.bfloat16
    slots = tokens // FIRST_DILATION
    return pl.pallas_call(
        functools.partial(kernel, chips),
        out_shape=jax.ShapeDtypeStruct((tokens, columns), bf16),
        in_specs=[pl.BlockSpec(memory_space=pl.ANY)] * 4,
        out_specs=pl.BlockSpec(memory_space=pl.ANY),
        scratch_shapes=[
            pltpu.VMEM(queries.shape, bf16),
            pltpu.VMEM(keys.shape, bf16),
            pltpu.VMEM(values.shape, bf16),
            pltpu.VMEM(out_weight.shape, bf16),
            pltpu.VMEM((tokens, columns), bf16),
            pltpu.VMEM((WIDTH, tokens), bf16),
            pltpu.VMEM((PAIRS, LANES, tokens), bf16),
            pltpu.VMEM((WIDTH, tokens), bf16),
            pltpu.VMEM((PAIRS, LANES, LANES), bf16),
            pltpu.VMEM((2, chips[0], slots, 2 * WIDTH), bf16),
            pltpu.VMEM((2, chips[1], slots // 4, 2 * WIDTH), bf16),
            pltpu.VMEM((2, chips[2], 16, 2 * LANES), bf16),
            pltpu.SemaphoreType.DMA((4,)),
            pltpu.SemaphoreType.DMA((tokens // QUERY_CHUNK,)),
            pltpu.SemaphoreType.DMA((3,)),
            pltpu.SemaphoreType.DMA((3,)),
            pltpu.SemaphoreType.DMA((3,)),
            pltpu.SemaphoreType.DMA((3,)),
        ],
        compiler_params=pltpu.CompilerParams(
            collective_id=0, has_side_effects=True, vmem_limit_bytes=56 * 1024 * 1024
        ),
        cost_estimate=pl.CostEstimate(
            flops=1_000_000_000, bytes_accessed=3_000_000, transcendentals=2_000_000
        ),
    )(queries, keys, values, out_weight)


def solution(mesh):
    in_specs = (P("seq", None), P("seq", None), P("seq", None), P())
    return jax.shard_map(
        on_device, mesh=mesh, in_specs=in_specs, out_specs=P("seq", None), check_vma=False
    )
```

```python
import functools
import math

import jax
import jax.numpy as jnp
from jax import lax
from jax.experimental import pallas as pl
from jax.experimental.pallas import tpu as pltpu
from jax.sharding import PartitionSpec as P

HEAD_COUNT = 6
HEAD_SIZE = 64
PAIRS = HEAD_COUNT // 2
FIRST_DILATION = 8
WIDTH = HEAD_COUNT * HEAD_SIZE
LANES = 2 * HEAD_SIZE
ABSENT = -1e30
SCALE = math.log2(math.e) / math.sqrt(HEAD_SIZE)
MESH = pl.DeviceIdType.MESH
VMEM_LIMIT = int(53.35 * 1024 * 1024)
QUERY_CHUNK = 256


def iota(shape, axis):
    return lax.broadcasted_iota(jnp.int32, shape, axis)


def one_hot_rows(pair, tokens):
    row = iota((LANES, 1), 0)
    half = row >> 6
    slot = row & 63
    turned = (slot - 4 * pair) & 15
    rest = turned - 4
    third = rest * 43 >> 7
    second_place = jnp.where(turned < 4, 16 * turned, 16 * third + 4 * (rest - 3 * third + 1))
    other = slot - 16
    third = other * 43 >> 7
    first_place = 4 * third + (other - 3 * third) + 1
    place = jnp.where(slot < 16, second_place, first_place)
    token = FIRST_DILATION * place + 2 * pair + half
    return jnp.where(iota((LANES, tokens), 1) == token, 1.0, 0.0).astype(jnp.bfloat16)


def dot(a, b, dims=((1,), (0,))):
    return lax.dot_general(a, b, (dims, ((), ())), preferred_element_type=jnp.float32)


def partial_softmax(scores, value, value_dim):
    top = jnp.max(scores, axis=0, keepdims=True)
    prob = jnp.exp2((scores - top) * SCALE)
    total = jnp.sum(prob, axis=0, keepdims=True)
    return top, total, dot(value, prob.astype(jnp.bfloat16), ((value_dim,), (0,)))


def join(parts):
    top = functools.reduce(jnp.maximum, [p[0] for p in parts])
    weights = [jnp.exp2((p[0] - top) * SCALE) for p in parts]
    total = sum(w * p[1] for w, p in zip(weights, parts))
    return sum(w * p[2] for w, p in zip(weights, parts)) * (1.0 / total)


def kernel(
    chips, q_hbm, k_hbm, v_hbm, out_hbm,
    q_ref, k_ref, v_ref, comb, spread, vt, qt, qbd, near, middle, whole,
    in_sem, out_sem, send_sem, recv_sem, mate_send, mate_recv,
):
    tokens = q_ref.shape[0]
    me = lax.axis_index("seq")
    chip = lax.div(me, 2)
    core = lax.rem(me, 2)
    mate = chip * 2 + 1 - core
    bufs = (near, middle, whole)

    loads = []
    for n, (src, dst) in enumerate(((k_hbm, k_ref), (v_hbm, v_ref), (q_hbm, q_ref))):
        loads.append(pltpu.make_async_copy(src, dst, in_sem.at[n]))
        loads[-1].start()

    barrier = pltpu.get_barrier_semaphore()
    pl.semaphore_signal(barrier, inc=1, device_id=(mate,), device_id_type=MESH)

    def over(count, body):
        if count <= 16:
            for d in range(1, count):
                body(d)
        else:
            lax.fori_loop(1, count, lambda d, _: (body(d), 0)[1], 0)

    def peer(count, d):
        place = lax.rem(chip, count)
        return (chip - place + lax.rem(place + d, count)) * 2 + core

    total_chips = chips[2]

    def greet(d):
        pl.semaphore_signal(
            barrier, inc=1, device_id=(peer(total_chips, d),), device_id_type=MESH
        )

    over(total_chips, greet)

    block_diagonal = (iota((LANES, LANES), 0) >> 6) == (iota((LANES, LANES), 1) >> 6)
    for t in range(PAIRS):
        spread[t] = one_hot_rows(t, tokens)

    places = [lax.rem(chip, c) for c in chips]
    slot_pair = iota((16, LANES), 0) >> 2
    for n, src in enumerate((k_ref, v_ref)):
        loads[n].wait()
        packed = jnp.zeros((16, LANES), jnp.float32)
        for t in range(PAIRS):
            picked = dot(spread[t], src[:, t * LANES:(t + 1) * LANES])
            picked = jnp.where(block_diagonal, picked, 0.0)
            rows = picked[:HEAD_SIZE] + picked[HEAD_SIZE:]
            packed = jnp.where(slot_pair == t, rows[:16], packed)
            rows = rows.astype(jnp.bfloat16)
            first = n * WIDTH + t * LANES
            near[core, places[0], :, first:first + LANES] = rows
            middle[core, places[1], :, first:first + LANES] = rows[:16]
        whole[core, places[2], :, n * LANES:(n + 1) * LANES] = packed.astype(jnp.bfloat16)

    pl.semaphore_wait(barrier, total_chips)

    for level in (2, 1, 0):
        own = bufs[level].at[core, places[level]]

        def send(d, level=level, own=own):
            pltpu.make_async_remote_copy(
                src_ref=own,
                dst_ref=own,
                send_sem=send_sem.at[level],
                recv_sem=recv_sem.at[level],
                device_id=(peer(chips[level], d),),
                device_id_type=MESH,
            ).start()

        over(chips[level], send)

    def to_mate(level):
        part = bufs[level].at[core]
        return pltpu.make_async_remote_copy(
            src_ref=part,
            dst_ref=part,
            send_sem=mate_send.at[level],
            recv_sem=mate_recv.at[level],
            device_id=(mate,),
            device_id_type=MESH,
        )

    def others(level, sem):
        part = bufs[level].at[core, pl.ds(0, chips[level] - 1)]
        return pltpu.make_async_copy(part, part, sem.at[level])

    def forward(level):
        if chips[level] > 1:
            others(level, recv_sem).wait()
        to_mate(level).start()

    if chips[0] == 1:
        forward(0)

    vt[...] = v_ref[...].T
    loads[2].wait()
    for t in range(PAIRS):
        picked = dot(spread[t], q_ref[:, t * LANES:(t + 1) * LANES])
        qbd[t] = jnp.where(block_diagonal, picked, 0.0).astype(jnp.bfloat16)

    for t in range(PAIRS):
        turned = q_ref[:, t * LANES:(t + 1) * LANES].T
        for e in range(2):
            mine = (iota(turned.shape, 0) >> 6) == e
            qt[2 * t + e] = jnp.where(mine, turned, jnp.zeros_like(turned))

    def local_heads(heads):
        chunks = [(h, first) for h in heads for first in range(0, tokens, QUERY_CHUNK)]

        def scores_of(chunk):
            h, first = chunk
            t = h // 2
            return dot(k_ref[:, t * LANES:(t + 1) * LANES], qt[h, :, first:first + QUERY_CHUNK])

        ahead = scores_of(chunks[0])
        for n, (h, first) in enumerate(chunks):
            scores = ahead
            if n + 1 < len(chunks):
                ahead = scores_of(chunks[n + 1])
            rows = slice(h * HEAD_SIZE, (h + 1) * HEAD_SIZE)
            _, total, out = partial_softmax(scores, vt[rows], 1)
            comb[rows, first:first + QUERY_CHUNK] = (out * (1.0 / total)).astype(jnp.bfloat16)

    local_heads(range(0, 3))
    for level in (1, 2) if chips[0] == 1 else (0, 1, 2):
        forward(level)
    local_heads(range(3, HEAD_COUNT))

    parts = []
    for t in range(PAIRS):
        columns = slice(t * LANES, (t + 1) * LANES)
        scores = dot(k_ref[:, columns], qbd[t], ((1,), (1,)))
        parts.append([partial_softmax(scores, vt[columns], 1)])

    def rows_of(buf, first):
        block = buf[:, :, :, first:first + LANES]
        return block.reshape(-1, LANES)

    def shared_level(buf, t):
        scores = dot(rows_of(buf, t * LANES), qbd[t], ((1,), (1,)))
        return partial_softmax(scores, rows_of(buf, WIDTH + t * LANES), 0)

    lane_slot = iota((1, LANES), 1) & 63
    slot_rows = (iota((LANES, LANES), 0) & 63) >> 2
    query = jnp.zeros((LANES, LANES), jnp.float32)
    for t in range(PAIRS):
        query = jnp.where(slot_rows == t, qbd[t].astype(jnp.float32), query)
    query = query.astype(jnp.bfloat16)

    to_mate(0).wait()
    for t in range(PAIRS):
        parts[t].append(shared_level(near, t))

    to_mate(1).wait()
    for t in range(PAIRS):
        top, total, out = shared_level(middle, t)
        parts[t].append((jnp.where(lane_slot < 16, top, ABSENT), total, out))

    to_mate(2).wait()
    scores = dot(rows_of(whole, 0), query, ((1,), (1,)))
    row_pair = (iota(scores.shape, 0) & 15) >> 2
    scores = jnp.where(row_pair == (lane_slot >> 2), scores, ABSENT)
    top3, total3, out3 = partial_softmax(scores, rows_of(whole, LANES), 0)

    stores = []
    for t in range(PAIRS):
        columns = slice(t * LANES, (t + 1) * LANES)
        parts[t].append((jnp.where((lane_slot >> 2) == t, top3, ABSENT), total3, out3))
        merged = jnp.where(block_diagonal, join(parts[t]), 0.0).astype(jnp.bfloat16)
        placed = dot(merged, spread[t])
        head = 2 * t + (iota(placed.shape, 0) >> 6)
        chosen = (iota(placed.shape, 1) & (FIRST_DILATION - 1)) == head
        comb[columns] = jnp.where(
            chosen, placed, comb[columns].astype(jnp.float32)
        ).astype(jnp.bfloat16)
        stores.append(pltpu.make_async_copy(comb.at[columns], out_hbm.at[columns], out_sem.at[t]))
        stores[-1].start()

    for level in range(3):
        if chips[level] > 1:
            others(level, send_sem).wait()
    for store in stores:
        store.wait()


def on_device(queries, keys, values, out_weight):
    devices = lax.axis_size("seq")
    tokens = queries.shape[0]
    chips = (devices // 32, devices // 8, devices // 2)
    bf16 = jnp.bfloat16
    slots = tokens // FIRST_DILATION
    combined = pl.pallas_call(
        functools.partial(kernel, chips),
        out_shape=jax.ShapeDtypeStruct((WIDTH, tokens), bf16),
        in_specs=[pl.BlockSpec(memory_space=pl.ANY)] * 3,
        out_specs=pl.BlockSpec(memory_space=pl.ANY),
        scratch_shapes=[
            pltpu.VMEM(queries.shape, bf16),
            pltpu.VMEM(keys.shape, bf16),
            pltpu.VMEM(values.shape, bf16),
            pltpu.VMEM((WIDTH, tokens), bf16),
            pltpu.VMEM((PAIRS, LANES, tokens), bf16),
            pltpu.VMEM((WIDTH, tokens), bf16),
            pltpu.VMEM((HEAD_COUNT, LANES, tokens), bf16),
            pltpu.VMEM((PAIRS, LANES, LANES), bf16),
            pltpu.VMEM((2, chips[0], slots, 2 * WIDTH), bf16),
            pltpu.VMEM((2, chips[1], slots // 4, 2 * WIDTH), bf16),
            pltpu.VMEM((2, chips[2], 16, 2 * LANES), bf16),
            pltpu.SemaphoreType.DMA((3,)),
            pltpu.SemaphoreType.DMA((PAIRS,)),
            pltpu.SemaphoreType.DMA((3,)),
            pltpu.SemaphoreType.DMA((3,)),
            pltpu.SemaphoreType.DMA((3,)),
            pltpu.SemaphoreType.DMA((3,)),
        ],
        compiler_params=pltpu.CompilerParams(
            collective_id=0, has_side_effects=True, vmem_limit_bytes=VMEM_LIMIT
        ),
        cost_estimate=pl.CostEstimate(
            flops=1_000_000_000, bytes_accessed=3_000_000, transcendentals=2_000_000
        ),
    )(queries, keys, values)
    return dot(combined, out_weight, ((0,), (0,))).astype(bf16)


def solution(mesh):
    in_specs = (P("seq", None), P("seq", None), P("seq", None), P())
    return jax.shard_map(
        on_device, mesh=mesh, in_specs=in_specs, out_specs=P("seq", None), check_vma=False
    )
```

```python
import functools
import math

import jax
import jax.numpy as jnp
from jax import lax
from jax.experimental import pallas as pl
from jax.experimental.pallas import tpu as pltpu
from jax.sharding import PartitionSpec as P

HEAD_COUNT = 6
HEAD_SIZE = 64
PAIRS = HEAD_COUNT // 2
FIRST_DILATION = 8
WIDTH = HEAD_COUNT * HEAD_SIZE
LANES = 2 * HEAD_SIZE
ABSENT = -1e30
SCALE = math.log2(math.e) / math.sqrt(HEAD_SIZE)
MESH = pl.DeviceIdType.MESH
HALF_FIRST = 4
ALL_FIRST = 1
VMEM_LIMIT = int(53.35 * 1024 * 1024)
QUERY_CHUNK = 256


def iota(shape, axis):
    return lax.broadcasted_iota(jnp.int32, shape, axis)


def one_hot_rows(pair, tokens):
    row = iota((LANES, 1), 0)
    half = row >> 6
    slot = row & 63
    turned = (slot - 4 * pair) & 15
    rest = turned - 4
    third = rest * 43 >> 7
    second_place = jnp.where(turned < 4, 16 * turned, 16 * third + 4 * (rest - 3 * third + 1))
    other = slot - 16
    third = other * 43 >> 7
    first_place = 4 * third + (other - 3 * third) + 1
    place = jnp.where(slot < 16, second_place, first_place)
    token = FIRST_DILATION * place + 2 * pair + half
    return jnp.where(iota((LANES, tokens), 1) == token, 1.0, 0.0).astype(jnp.bfloat16)


def dot(a, b, dims=((1,), (0,))):
    return lax.dot_general(a, b, (dims, ((), ())), preferred_element_type=jnp.float32)


def partial_softmax(scores, value, value_dim):
    top = jnp.max(scores, axis=0, keepdims=True)
    prob = jnp.exp2((scores - top) * SCALE)
    total = jnp.sum(prob, axis=0, keepdims=True)
    return top, total, dot(value, prob.astype(jnp.bfloat16), ((value_dim,), (0,)))


def join(a, b):
    top = jnp.maximum(a[0], b[0])
    a_weight = jnp.exp2((a[0] - top) * SCALE)
    b_weight = jnp.exp2((b[0] - top) * SCALE)
    return top, a_weight * a[1] + b_weight * b[1], a_weight * a[2] + b_weight * b[2]


def kernel(
    chips, q_hbm, k_hbm, v_hbm, out_hbm,
    q_ref, k_ref, v_ref, comb, spread, vt, qt, qbd, tops, totals, sums, near, middle, whole,
    in_sem, out_sem, send_sem, recv_sem, mate_send, mate_recv,
):
    tokens = q_ref.shape[0]
    me = lax.axis_index("seq")
    chip = lax.div(me, 2)
    core = lax.rem(me, 2)
    mate = chip * 2 + 1 - core
    bufs = (near, middle, whole)

    loads = []
    for n, (src, dst) in enumerate(((k_hbm, k_ref), (v_hbm, v_ref), (q_hbm, q_ref))):
        loads.append(pltpu.make_async_copy(src, dst, in_sem.at[n]))
        loads[-1].start()

    barrier = pltpu.get_barrier_semaphore()
    pl.semaphore_signal(barrier, inc=1, device_id=(mate,), device_id_type=MESH)

    def over(count, body):
        if count <= 16:
            for d in range(1, count):
                body(d)
        else:
            lax.fori_loop(1, count, lambda d, _: (body(d), 0)[1], 0)

    def peer(count, d):
        place = lax.rem(chip, count)
        return (chip - place + d - jnp.where(d <= place, 1, 0)) * 2 + core

    total_chips = chips[2]

    def greet(d):
        pl.semaphore_signal(
            barrier, inc=1, device_id=(peer(total_chips, d),), device_id_type=MESH
        )

    over(total_chips, greet)

    block_diagonal = (iota((LANES, LANES), 0) >> 6) == (iota((LANES, LANES), 1) >> 6)
    for t in range(PAIRS):
        spread[t] = one_hot_rows(t, tokens)

    places = [lax.rem(chip, c) for c in chips]
    slot_pair = iota((16, LANES), 0) >> 2
    for n, src in enumerate((k_ref, v_ref)):
        loads[n].wait()
        packed = jnp.zeros((16, LANES), jnp.float32)
        for t in range(PAIRS):
            picked = dot(spread[t], src[:, t * LANES:(t + 1) * LANES])
            picked = jnp.where(block_diagonal, picked, 0.0)
            rows = picked[:HEAD_SIZE] + picked[HEAD_SIZE:]
            packed = jnp.where(slot_pair == t, rows[:16], packed)
            rows = rows.astype(jnp.bfloat16)
            first = n * WIDTH + t * LANES
            near[core, places[0], :, first:first + LANES] = rows
            middle[core, places[1], :, first:first + LANES] = rows[:16]
        whole[core, places[2], :, n * LANES:(n + 1) * LANES] = packed.astype(jnp.bfloat16)

    def prepare():
        vt[...] = v_ref[...].T
        loads[2].wait()
        for t in range(PAIRS):
            picked = dot(spread[t], q_ref[:, t * LANES:(t + 1) * LANES])
            qbd[t] = jnp.where(block_diagonal, picked, 0.0).astype(jnp.bfloat16)

        for t in range(PAIRS):
            turned = q_ref[:, t * LANES:(t + 1) * LANES].T
            for e in range(2):
                mine = (iota(turned.shape, 0) >> 6) == e
                qt[2 * t + e] = jnp.where(mine, turned, jnp.zeros_like(turned))

    def local_heads(heads):
        chunks = [(h, first) for h in heads for first in range(0, tokens, QUERY_CHUNK)]

        def scores_of(chunk):
            h, first = chunk
            t = h // 2
            return dot(k_ref[:, t * LANES:(t + 1) * LANES], qt[h, :, first:first + QUERY_CHUNK])

        ahead = scores_of(chunks[0])
        for n, (h, first) in enumerate(chunks):
            scores = ahead
            if n + 1 < len(chunks):
                ahead = scores_of(chunks[n + 1])
            rows = slice(h * HEAD_SIZE, (h + 1) * HEAD_SIZE)
            _, total, out = partial_softmax(scores, vt[rows], 1)
            comb[rows, first:first + QUERY_CHUNK] = (out * (1.0 / total)).astype(jnp.bfloat16)

    def first_half():
        prepare()
        local_heads(range(0, 3))

    def second_half():
        local_heads(range(3, HEAD_COUNT))
        for t in range(PAIRS):
            columns = slice(t * LANES, (t + 1) * LANES)
            scores = dot(k_ref[:, columns], qbd[t], ((1,), (1,)))
            top, total, out = partial_softmax(scores, vt[columns], 1)
            tops[t], totals[t], sums[t] = top, total, out

    def before(bound, work):
        pl.when(chip < bound)(work)

    def after(bound, work):
        pl.when(chip >= bound)(work)

    before(HALF_FIRST, first_half)
    before(ALL_FIRST, second_half)

    pl.semaphore_wait(barrier, total_chips)

    for level in (2, 1, 0):
        own = bufs[level].at[core, places[level]]

        def send(d, level=level, own=own):
            pltpu.make_async_remote_copy(
                src_ref=own,
                dst_ref=own,
                send_sem=send_sem.at[level],
                recv_sem=recv_sem.at[level],
                device_id=(peer(chips[level], d),),
                device_id_type=MESH,
            ).start()

        over(chips[level], send)

    def to_mate(level):
        part = bufs[level].at[core]
        return pltpu.make_async_remote_copy(
            src_ref=part,
            dst_ref=part,
            send_sem=mate_send.at[level],
            recv_sem=mate_recv.at[level],
            device_id=(mate,),
            device_id_type=MESH,
        )

    def others(level, sem):
        part = bufs[level].at[core, pl.ds(0, chips[level] - 1)]
        return pltpu.make_async_copy(part, part, sem.at[level])

    def forward(level):
        if chips[level] > 1:
            others(level, recv_sem).wait()
        to_mate(level).start()

    if chips[0] == 1:
        forward(0)

    after(HALF_FIRST, first_half)
    if chips[0] > 1:
        forward(0)
    after(ALL_FIRST, second_half)
    forward(1)
    forward(2)

    def rows_of(buf, first):
        block = buf[:, :, :, first:first + LANES]
        return block.reshape(-1, LANES)

    def shared_level(buf, t):
        scores = dot(rows_of(buf, t * LANES), qbd[t], ((1,), (1,)))
        return partial_softmax(scores, rows_of(buf, WIDTH + t * LANES), 0)

    lane_slot = iota((1, LANES), 1) & 63
    slot_rows = (iota((LANES, LANES), 0) & 63) >> 2
    query = jnp.zeros((LANES, LANES), jnp.float32)
    for t in range(PAIRS):
        query = jnp.where(slot_rows == t, qbd[t].astype(jnp.float32), query)
    query = query.astype(jnp.bfloat16)

    to_mate(0).wait()
    for t in range(PAIRS):
        done = (tops[t], totals[t], sums[t])
        tops[t], totals[t], sums[t] = join(done, shared_level(near, t))

    to_mate(1).wait()
    for t in range(PAIRS):
        top, total, out = shared_level(middle, t)
        done = (tops[t], totals[t], sums[t])
        part = (jnp.where(lane_slot < 16, top, ABSENT), total, out)
        tops[t], totals[t], sums[t] = join(done, part)

    to_mate(2).wait()
    scores = dot(rows_of(whole, 0), query, ((1,), (1,)))
    row_pair = (iota(scores.shape, 0) & 15) >> 2
    scores = jnp.where(row_pair == (lane_slot >> 2), scores, ABSENT)
    top3, total3, out3 = partial_softmax(scores, rows_of(whole, LANES), 0)

    stores = []
    for t in range(PAIRS):
        columns = slice(t * LANES, (t + 1) * LANES)
        part = (jnp.where((lane_slot >> 2) == t, top3, ABSENT), total3, out3)
        _, total, out = join((tops[t], totals[t], sums[t]), part)
        merged = jnp.where(block_diagonal, out * (1.0 / total), 0.0).astype(jnp.bfloat16)
        placed = dot(merged, spread[t])
        head = 2 * t + (iota(placed.shape, 0) >> 6)
        chosen = (iota(placed.shape, 1) & (FIRST_DILATION - 1)) == head
        comb[columns] = jnp.where(
            chosen, placed, comb[columns].astype(jnp.float32)
        ).astype(jnp.bfloat16)
        stores.append(pltpu.make_async_copy(comb.at[columns], out_hbm.at[columns], out_sem.at[t]))
        stores[-1].start()

    for level in range(3):
        if chips[level] > 1:
            others(level, send_sem).wait()
    for store in stores:
        store.wait()


def on_device(queries, keys, values, out_weight):
    devices = lax.axis_size("seq")
    tokens = queries.shape[0]
    chips = (devices // 32, devices // 8, devices // 2)
    bf16 = jnp.bfloat16
    slots = tokens // FIRST_DILATION
    combined = pl.pallas_call(
        functools.partial(kernel, chips),
        out_shape=jax.ShapeDtypeStruct((WIDTH, tokens), bf16),
        in_specs=[pl.BlockSpec(memory_space=pl.ANY)] * 3,
        out_specs=pl.BlockSpec(memory_space=pl.ANY),
        scratch_shapes=[
            pltpu.VMEM(queries.shape, bf16),
            pltpu.VMEM(keys.shape, bf16),
            pltpu.VMEM(values.shape, bf16),
            pltpu.VMEM((WIDTH, tokens), bf16),
            pltpu.VMEM((PAIRS, LANES, tokens), bf16),
            pltpu.VMEM((WIDTH, tokens), bf16),
            pltpu.VMEM((HEAD_COUNT, LANES, tokens), bf16),
            pltpu.VMEM((PAIRS, LANES, LANES), bf16),
            pltpu.VMEM((PAIRS, 1, LANES), jnp.float32),
            pltpu.VMEM((PAIRS, 1, LANES), jnp.float32),
            pltpu.VMEM((PAIRS, LANES, LANES), jnp.float32),
            pltpu.VMEM((2, chips[0], slots, 2 * WIDTH), bf16),
            pltpu.VMEM((2, chips[1], slots // 4, 2 * WIDTH), bf16),
            pltpu.VMEM((2, chips[2], 16, 2 * LANES), bf16),
            pltpu.SemaphoreType.DMA((3,)),
            pltpu.SemaphoreType.DMA((PAIRS,)),
            pltpu.SemaphoreType.DMA((3,)),
            pltpu.SemaphoreType.DMA((3,)),
            pltpu.SemaphoreType.DMA((3,)),
            pltpu.SemaphoreType.DMA((3,)),
        ],
        compiler_params=pltpu.CompilerParams(
            collective_id=0, has_side_effects=True, vmem_limit_bytes=VMEM_LIMIT
        ),
        cost_estimate=pl.CostEstimate(
            flops=1_000_000_000, bytes_accessed=3_000_000, transcendentals=2_000_000
        ),
    )(queries, keys, values)
    return dot(combined, out_weight, ((0,), (0,))).astype(bf16)


def solution(mesh):
    in_specs = (P("seq", None), P("seq", None), P("seq", None), P())
    return jax.shard_map(
        on_device, mesh=mesh, in_specs=in_specs, out_specs=P("seq", None), check_vma=False
    )
```

```python
import functools
import math

import jax
import jax.numpy as jnp
from jax import lax
from jax.experimental import pallas as pl
from jax.experimental.pallas import tpu as pltpu
from jax.sharding import PartitionSpec as P

HEAD_COUNT = 6
HEAD_SIZE = 64
PAIRS = HEAD_COUNT // 2
FIRST_DILATION = 8
WIDTH = HEAD_COUNT * HEAD_SIZE
LANES = 2 * HEAD_SIZE
ABSENT = -1e30
SCALE = math.log2(math.e) / math.sqrt(HEAD_SIZE)
MESH = pl.DeviceIdType.MESH
HALF_FIRST = 4
ALL_FIRST = 1
VMEM_LIMIT = int(53.35 * 1024 * 1024)
QUERY_CHUNK = 256


def iota(shape, axis):
    return lax.broadcasted_iota(jnp.int32, shape, axis)


def one_hot_rows(pair, tokens):
    row = iota((LANES, 1), 0)
    half = row >> 6
    slot = row & 63
    turned = (slot - 4 * pair) & 15
    rest = turned - 4
    third = rest * 43 >> 7
    second_place = jnp.where(turned < 4, 16 * turned, 16 * third + 4 * (rest - 3 * third + 1))
    other = slot - 16
    third = other * 43 >> 7
    first_place = 4 * third + (other - 3 * third) + 1
    place = jnp.where(slot < 16, second_place, first_place)
    token = FIRST_DILATION * place + 2 * pair + half
    return jnp.where(iota((LANES, tokens), 1) == token, 1.0, 0.0).astype(jnp.bfloat16)


def dot(a, b, dims=((1,), (0,))):
    return lax.dot_general(a, b, (dims, ((), ())), preferred_element_type=jnp.float32)


def partial_softmax(scores, value, value_dim):
    top = jnp.max(scores, axis=0, keepdims=True)
    prob = jnp.exp2((scores - top) * SCALE)
    total = jnp.sum(prob, axis=0, keepdims=True)
    return top, total, dot(value, prob.astype(jnp.bfloat16), ((value_dim,), (0,)))


def join(a, b):
    top = jnp.maximum(a[0], b[0])
    a_weight = jnp.exp2((a[0] - top) * SCALE)
    b_weight = jnp.exp2((b[0] - top) * SCALE)
    return top, a_weight * a[1] + b_weight * b[1], a_weight * a[2] + b_weight * b[2]


def kernel(
    chips, q_hbm, k_hbm, v_hbm, comb,
    q_ref, k_ref, v_ref, spread, vt, qt, qbd, tops, totals, sums, near, middle, whole,
    in_sem, send_sem, recv_sem, mate_send, mate_recv,
):
    tokens = q_ref.shape[0]
    me = lax.axis_index("seq")
    chip = lax.div(me, 2)
    core = lax.rem(me, 2)
    mate = chip * 2 + 1 - core
    bufs = (near, middle, whole)

    loads = []
    for n, (src, dst) in enumerate(((k_hbm, k_ref), (v_hbm, v_ref), (q_hbm, q_ref))):
        loads.append(pltpu.make_async_copy(src, dst, in_sem.at[n]))
        loads[-1].start()

    barrier = pltpu.get_barrier_semaphore()
    pl.semaphore_signal(barrier, inc=1, device_id=(mate,), device_id_type=MESH)

    def over(count, body):
        if count <= 16:
            for d in range(1, count):
                body(d)
        else:
            lax.fori_loop(1, count, lambda d, _: (body(d), 0)[1], 0)

    def peer(count, d):
        place = lax.rem(chip, count)
        return (chip - place + d - jnp.where(d <= place, 1, 0)) * 2 + core

    total_chips = chips[2]

    def greet(d):
        pl.semaphore_signal(
            barrier, inc=1, device_id=(peer(total_chips, d),), device_id_type=MESH
        )

    over(total_chips, greet)

    block_diagonal = (iota((LANES, LANES), 0) >> 6) == (iota((LANES, LANES), 1) >> 6)
    for t in range(PAIRS):
        spread[t] = one_hot_rows(t, tokens)

    places = [lax.rem(chip, c) for c in chips]
    slot_pair = iota((16, LANES), 0) >> 2
    for n, src in enumerate((k_ref, v_ref)):
        loads[n].wait()
        packed = jnp.zeros((16, LANES), jnp.float32)
        for t in range(PAIRS):
            picked = dot(spread[t], src[:, t * LANES:(t + 1) * LANES])
            picked = jnp.where(block_diagonal, picked, 0.0)
            rows = picked[:HEAD_SIZE] + picked[HEAD_SIZE:]
            packed = jnp.where(slot_pair == t, rows[:16], packed)
            rows = rows.astype(jnp.bfloat16)
            first = n * WIDTH + t * LANES
            near[core, places[0], :, first:first + LANES] = rows
            middle[core, places[1], :, first:first + LANES] = rows[:16]
        whole[core, places[2], :, n * LANES:(n + 1) * LANES] = packed.astype(jnp.bfloat16)

    def prepare():
        vt[...] = v_ref[...].T
        loads[2].wait()
        for t in range(PAIRS):
            picked = dot(spread[t], q_ref[:, t * LANES:(t + 1) * LANES])
            qbd[t] = jnp.where(block_diagonal, picked, 0.0).astype(jnp.bfloat16)

        for t in range(PAIRS):
            turned = q_ref[:, t * LANES:(t + 1) * LANES].T
            for e in range(2):
                mine = (iota(turned.shape, 0) >> 6) == e
                qt[2 * t + e] = jnp.where(mine, turned, jnp.zeros_like(turned))

    def local_heads(heads):
        chunks = [(h, first) for h in heads for first in range(0, tokens, QUERY_CHUNK)]

        def scores_of(chunk):
            h, first = chunk
            t = h // 2
            return dot(k_ref[:, t * LANES:(t + 1) * LANES], qt[h, :, first:first + QUERY_CHUNK])

        ahead = scores_of(chunks[0])
        for n, (h, first) in enumerate(chunks):
            scores = ahead
            if n + 1 < len(chunks):
                ahead = scores_of(chunks[n + 1])
            rows = slice(h * HEAD_SIZE, (h + 1) * HEAD_SIZE)
            _, total, out = partial_softmax(scores, vt[rows], 1)
            comb[rows, first:first + QUERY_CHUNK] = (out * (1.0 / total)).astype(jnp.bfloat16)

    def first_half():
        prepare()
        local_heads(range(0, 3))

    def second_half():
        local_heads(range(3, HEAD_COUNT))
        for t in range(PAIRS):
            columns = slice(t * LANES, (t + 1) * LANES)
            scores = dot(k_ref[:, columns], qbd[t], ((1,), (1,)))
            top, total, out = partial_softmax(scores, vt[columns], 1)
            tops[t], totals[t], sums[t] = top, total, out

    def before(bound, work):
        pl.when(chip < bound)(work)

    def after(bound, work):
        pl.when(chip >= bound)(work)

    before(HALF_FIRST, first_half)
    before(ALL_FIRST, second_half)

    pl.semaphore_wait(barrier, total_chips)

    for level in (1, 2, 0):
        own = bufs[level].at[core, places[level]]

        def send(d, level=level, own=own):
            pltpu.make_async_remote_copy(
                src_ref=own,
                dst_ref=own,
                send_sem=send_sem.at[level],
                recv_sem=recv_sem.at[level],
                device_id=(peer(chips[level], d),),
                device_id_type=MESH,
            ).start()

        over(chips[level], send)

    def to_mate(level):
        part = bufs[level].at[core]
        return pltpu.make_async_remote_copy(
            src_ref=part,
            dst_ref=part,
            send_sem=mate_send.at[level],
            recv_sem=mate_recv.at[level],
            device_id=(mate,),
            device_id_type=MESH,
        )

    def others(level, sem):
        part = bufs[level].at[core, pl.ds(0, chips[level] - 1)]
        return pltpu.make_async_copy(part, part, sem.at[level])

    def forward(level):
        if chips[level] > 1:
            others(level, recv_sem).wait()
        to_mate(level).start()

    if chips[0] == 1:
        forward(0)

    after(HALF_FIRST, first_half)
    if chips[0] > 1:
        forward(0)
    after(ALL_FIRST, second_half)

    def rows_of(buf, first):
        block = buf[:, :, :, first:first + LANES]
        return block.reshape(-1, LANES)

    def shared_level(buf, t):
        scores = dot(rows_of(buf, t * LANES), qbd[t], ((1,), (1,)))
        return partial_softmax(scores, rows_of(buf, WIDTH + t * LANES), 0)

    lane_slot = iota((1, LANES), 1) & 63
    slot_rows = (iota((LANES, LANES), 0) & 63) >> 2
    query = jnp.zeros((LANES, LANES), jnp.float32)
    for t in range(PAIRS):
        query = jnp.where(slot_rows == t, qbd[t].astype(jnp.float32), query)
    query = query.astype(jnp.bfloat16)

    to_mate(0).wait_recv()
    for t in range(PAIRS):
        done = (tops[t], totals[t], sums[t])
        tops[t], totals[t], sums[t] = join(done, shared_level(near, t))

    forward(1)
    forward(2)

    to_mate(1).wait_recv()
    for t in range(PAIRS):
        top, total, out = shared_level(middle, t)
        done = (tops[t], totals[t], sums[t])
        part = (jnp.where(lane_slot < 16, top, ABSENT), total, out)
        tops[t], totals[t], sums[t] = join(done, part)

    to_mate(2).wait_recv()
    scores = dot(rows_of(whole, 0), query, ((1,), (1,)))
    row_pair = (iota(scores.shape, 0) & 15) >> 2
    scores = jnp.where(row_pair == (lane_slot >> 2), scores, ABSENT)
    top3, total3, out3 = partial_softmax(scores, rows_of(whole, LANES), 0)

    for t in range(PAIRS):
        columns = slice(t * LANES, (t + 1) * LANES)
        part = (jnp.where((lane_slot >> 2) == t, top3, ABSENT), total3, out3)
        _, total, out = join((tops[t], totals[t], sums[t]), part)
        merged = jnp.where(block_diagonal, out * (1.0 / total), 0.0).astype(jnp.bfloat16)
        placed = dot(merged, spread[t])
        head = 2 * t + (iota(placed.shape, 0) >> 6)
        chosen = (iota(placed.shape, 1) & (FIRST_DILATION - 1)) == head
        comb[columns] = jnp.where(
            chosen, placed, comb[columns].astype(jnp.float32)
        ).astype(jnp.bfloat16)

    for level in range(3):
        to_mate(level).wait_send()
        if chips[level] > 1:
            others(level, send_sem).wait()


def on_device(queries, keys, values, out_weight):
    devices = lax.axis_size("seq")
    tokens = queries.shape[0]
    chips = (devices // 32, devices // 8, devices // 2)
    bf16 = jnp.bfloat16
    slots = tokens // FIRST_DILATION
    combined = pl.pallas_call(
        functools.partial(kernel, chips),
        out_shape=jax.ShapeDtypeStruct((WIDTH, tokens), bf16),
        in_specs=[pl.BlockSpec(memory_space=pl.ANY)] * 3,
        out_specs=pl.BlockSpec(memory_space=pltpu.VMEM),
        scratch_shapes=[
            pltpu.VMEM(queries.shape, bf16),
            pltpu.VMEM(keys.shape, bf16),
            pltpu.VMEM(values.shape, bf16),
            pltpu.VMEM((PAIRS, LANES, tokens), bf16),
            pltpu.VMEM((WIDTH, tokens), bf16),
            pltpu.VMEM((HEAD_COUNT, LANES, tokens), bf16),
            pltpu.VMEM((PAIRS, LANES, LANES), bf16),
            pltpu.VMEM((PAIRS, 1, LANES), jnp.float32),
            pltpu.VMEM((PAIRS, 1, LANES), jnp.float32),
            pltpu.VMEM((PAIRS, LANES, LANES), jnp.float32),
            pltpu.VMEM((2, chips[0], slots, 2 * WIDTH), bf16),
            pltpu.VMEM((2, chips[1], slots // 4, 2 * WIDTH), bf16),
            pltpu.VMEM((2, chips[2], 16, 2 * LANES), bf16),
            pltpu.SemaphoreType.DMA((3,)),
            pltpu.SemaphoreType.DMA((3,)),
            pltpu.SemaphoreType.DMA((3,)),
            pltpu.SemaphoreType.DMA((3,)),
            pltpu.SemaphoreType.DMA((3,)),
        ],
        compiler_params=pltpu.CompilerParams(
            collective_id=0, has_side_effects=True, vmem_limit_bytes=VMEM_LIMIT
        ),
        cost_estimate=pl.CostEstimate(
            flops=1_000_000_000, bytes_accessed=3_000_000, transcendentals=2_000_000
        ),
    )(queries, keys, values)
    return dot(combined, out_weight, ((0,), (0,))).astype(bf16)


def solution(mesh):
    in_specs = (P("seq", None), P("seq", None), P("seq", None), P())
    return jax.shard_map(
        on_device, mesh=mesh, in_specs=in_specs, out_specs=P("seq", None), check_vma=False
    )
```

```python
import functools
import math

import jax
import jax.numpy as jnp
from jax import lax
from jax.experimental import pallas as pl
from jax.experimental.pallas import tpu as pltpu
from jax.sharding import PartitionSpec as P

HEAD_COUNT = 6
HEAD_SIZE = 64
PAIRS = HEAD_COUNT // 2
FIRST_DILATION = 8
WIDTH = HEAD_COUNT * HEAD_SIZE
LANES = 2 * HEAD_SIZE
ABSENT = -1e30
SCALE = math.log2(math.e) / math.sqrt(HEAD_SIZE)
MESH = pl.DeviceIdType.MESH
HALF_FIRST = 4
ALL_FIRST = 1
VMEM_LIMIT = int(53.35 * 1024 * 1024)
QUERY_CHUNK = 256


def iota(shape, axis):
    return lax.broadcasted_iota(jnp.int32, shape, axis)


def one_hot_rows(pair, tokens):
    row = iota((LANES, 1), 0)
    half = row >> 6
    slot = row & 63
    turned = (slot - 4 * pair) & 15
    rest = turned - 4
    third = rest * 43 >> 7
    second_place = jnp.where(turned < 4, 16 * turned, 16 * third + 4 * (rest - 3 * third + 1))
    other = slot - 16
    third = other * 43 >> 7
    first_place = 4 * third + (other - 3 * third) + 1
    place = jnp.where(slot < 16, second_place, first_place)
    token = FIRST_DILATION * place + 2 * pair + half
    return jnp.where(iota((LANES, tokens), 1) == token, 1.0, 0.0).astype(jnp.bfloat16)


def dot(a, b, dims=((1,), (0,))):
    return lax.dot_general(a, b, (dims, ((), ())), preferred_element_type=jnp.float32)


def partial_softmax(scores, value, value_dim):
    top = jnp.max(scores, axis=0, keepdims=True)
    prob = jnp.exp2((scores - top) * SCALE)
    total = jnp.sum(prob, axis=0, keepdims=True)
    return top, total, dot(value, prob.astype(jnp.bfloat16), ((value_dim,), (0,)))


def join(a, b):
    top = jnp.maximum(a[0], b[0])
    a_weight = jnp.exp2((a[0] - top) * SCALE)
    b_weight = jnp.exp2((b[0] - top) * SCALE)
    return top, a_weight * a[1] + b_weight * b[1], a_weight * a[2] + b_weight * b[2]


def kernel(
    chips, q_hbm, k_hbm, v_hbm, comb,
    q_ref, k_ref, v_ref, spread, vt, qt, qbd, tops, totals, sums, near, middle, whole,
    in_sem, send_sem, recv_sem, mate_send, mate_recv,
):
    tokens = q_ref.shape[0]
    me = lax.axis_index("seq")
    chip = lax.div(me, 2)
    core = lax.rem(me, 2)
    mate = chip * 2 + 1 - core
    bufs = (near, middle, whole)

    loads = []
    for n, (src, dst) in enumerate(((k_hbm, k_ref), (v_hbm, v_ref), (q_hbm, q_ref))):
        loads.append(pltpu.make_async_copy(src, dst, in_sem.at[n]))
        loads[-1].start()

    barrier = pltpu.get_barrier_semaphore()
    pl.semaphore_signal(barrier, inc=1, device_id=(mate,), device_id_type=MESH)

    def over(count, body):
        if count <= 16:
            for d in range(1, count):
                body(d)
        else:
            lax.fori_loop(1, count, lambda d, _: (body(d), 0)[1], 0)

    def peer(count, d):
        place = lax.rem(chip, count)
        return (chip - place + d - jnp.where(d <= place, 1, 0)) * 2 + core

    total_chips = chips[2]

    def greet(d):
        pl.semaphore_signal(
            barrier, inc=1, device_id=(peer(total_chips, d),), device_id_type=MESH
        )

    over(total_chips, greet)

    block_diagonal = (iota((LANES, LANES), 0) >> 6) == (iota((LANES, LANES), 1) >> 6)
    for t in range(PAIRS):
        spread[t] = one_hot_rows(t, tokens)

    places = [lax.rem(chip, c) for c in chips]
    slot_pair = iota((16, LANES), 0) >> 2
    for n, src in enumerate((k_ref, v_ref)):
        loads[n].wait()
        packed = jnp.zeros((16, LANES), jnp.float32)
        for t in range(PAIRS):
            picked = dot(spread[t], src[:, t * LANES:(t + 1) * LANES])
            picked = jnp.where(block_diagonal, picked, 0.0)
            rows = picked[:HEAD_SIZE] + picked[HEAD_SIZE:]
            packed = jnp.where(slot_pair == t, rows[:16], packed)
            rows = rows.astype(jnp.bfloat16)
            first = n * WIDTH + t * LANES
            near[core, places[0], :, first:first + LANES] = rows
            middle[core, places[1], :, first:first + LANES] = rows[:16]
        whole[core, places[2], :, n * LANES:(n + 1) * LANES] = packed.astype(jnp.bfloat16)

    def prepare():
        vt[...] = v_ref[...].T
        loads[2].wait()
        for t in range(PAIRS):
            picked = dot(spread[t], q_ref[:, t * LANES:(t + 1) * LANES])
            qbd[t] = jnp.where(block_diagonal, picked, 0.0).astype(jnp.bfloat16)

        for t in range(PAIRS):
            turned = q_ref[:, t * LANES:(t + 1) * LANES].T
            for e in range(2):
                mine = (iota(turned.shape, 0) >> 6) == e
                qt[2 * t + e] = jnp.where(mine, turned, jnp.zeros_like(turned))

    def local_heads(heads):
        chunks = [(h, first) for h in heads for first in range(0, tokens, QUERY_CHUNK)]

        def scores_of(chunk):
            h, first = chunk
            t = h // 2
            return dot(k_ref[:, t * LANES:(t + 1) * LANES], qt[h, :, first:first + QUERY_CHUNK])

        ahead = scores_of(chunks[0])
        for n, (h, first) in enumerate(chunks):
            scores = ahead
            if n + 1 < len(chunks):
                ahead = scores_of(chunks[n + 1])
            rows = slice(h * HEAD_SIZE, (h + 1) * HEAD_SIZE)
            _, total, out = partial_softmax(scores, vt[rows], 1)
            comb[rows, first:first + QUERY_CHUNK] = (out * (1.0 / total)).astype(jnp.bfloat16)

    def first_half():
        prepare()
        local_heads(range(0, 3))

    def second_half():
        local_heads(range(3, HEAD_COUNT))
        for t in range(PAIRS):
            columns = slice(t * LANES, (t + 1) * LANES)
            scores = dot(k_ref[:, columns], qbd[t], ((1,), (1,)))
            top, total, out = partial_softmax(scores, vt[columns], 1)
            tops[t], totals[t], sums[t] = top, total, out

    def before(bound, work):
        pl.when(chip < bound)(work)

    def after(bound, work):
        pl.when(chip >= bound)(work)

    before(HALF_FIRST, first_half)
    before(ALL_FIRST, second_half)

    pl.semaphore_wait(barrier, total_chips)

    for level in (1, 2, 0):
        own = bufs[level].at[core, places[level]]

        def send(d, level=level, own=own):
            pltpu.make_async_remote_copy(
                src_ref=own,
                dst_ref=own,
                send_sem=send_sem.at[level],
                recv_sem=recv_sem.at[level],
                device_id=(peer(chips[level], d),),
                device_id_type=MESH,
            ).start()

        over(chips[level], send)

    def to_mate(level):
        part = bufs[level].at[core]
        return pltpu.make_async_remote_copy(
            src_ref=part,
            dst_ref=part,
            send_sem=mate_send.at[level],
            recv_sem=mate_recv.at[level],
            device_id=(mate,),
            device_id_type=MESH,
        )

    def others(level, sem):
        part = bufs[level].at[core, pl.ds(0, chips[level] - 1)]
        return pltpu.make_async_copy(part, part, sem.at[level])

    def forward(level):
        if chips[level] > 1:
            others(level, recv_sem).wait()
        to_mate(level).start()

    if chips[0] == 1:
        forward(0)

    after(HALF_FIRST, first_half)
    if chips[0] > 1:
        forward(0)
    after(ALL_FIRST, second_half)

    def rows_of(buf, first):
        block = buf[:, :, :, first:first + LANES]
        return block.reshape(-1, LANES)

    def shared_level(buf, t):
        scores = dot(rows_of(buf, t * LANES), qbd[t], ((1,), (1,)))
        return partial_softmax(scores, rows_of(buf, WIDTH + t * LANES), 0)

    lane_slot = iota((1, LANES), 1) & 63
    slot_rows = (iota((LANES, LANES), 0) & 63) >> 2
    query = jnp.zeros((LANES, LANES), jnp.float32)
    for t in range(PAIRS):
        query = jnp.where(slot_rows == t, qbd[t].astype(jnp.float32), query)
    query = query.astype(jnp.bfloat16)

    to_mate(0).wait_recv()
    for t in range(PAIRS):
        done = (tops[t], totals[t], sums[t])
        tops[t], totals[t], sums[t] = join(done, shared_level(near, t))

    forward(1)
    forward(2)

    to_mate(1).wait_recv()
    for t in range(PAIRS):
        top, total, out = shared_level(middle, t)
        done = (tops[t], totals[t], sums[t])
        part = (jnp.where(lane_slot < 16, top, ABSENT), total, out)
        tops[t], totals[t], sums[t] = join(done, part)

    for t in range(PAIRS):
        columns = slice(t * LANES, (t + 1) * LANES)
        head = 2 * t + (iota((LANES, tokens), 0) >> 6)
        chosen = (iota((LANES, tokens), 1) & (FIRST_DILATION - 1)) == head
        alone = comb[columns].astype(jnp.float32)
        comb[columns] = jnp.where(chosen, 0.0, alone).astype(jnp.bfloat16)

    to_mate(2).wait_recv()
    scores = dot(rows_of(whole, 0), query, ((1,), (1,)))
    row_pair = (iota(scores.shape, 0) & 15) >> 2
    scores = jnp.where(row_pair == (lane_slot >> 2), scores, ABSENT)
    top3, total3, out3 = partial_softmax(scores, rows_of(whole, LANES), 0)

    for t in range(PAIRS):
        columns = slice(t * LANES, (t + 1) * LANES)
        part = (jnp.where((lane_slot >> 2) == t, top3, ABSENT), total3, out3)
        _, total, out = join((tops[t], totals[t], sums[t]), part)
        merged = jnp.where(block_diagonal, out * (1.0 / total), 0.0).astype(jnp.bfloat16)
        placed = dot(merged, spread[t])
        comb[columns] = (comb[columns].astype(jnp.float32) + placed).astype(jnp.bfloat16)

    for level in range(3):
        to_mate(level).wait_send()
        if chips[level] > 1:
            others(level, send_sem).wait()


def on_device(queries, keys, values, out_weight):
    devices = lax.axis_size("seq")
    tokens = queries.shape[0]
    chips = (devices // 32, devices // 8, devices // 2)
    bf16 = jnp.bfloat16
    slots = tokens // FIRST_DILATION
    combined = pl.pallas_call(
        functools.partial(kernel, chips),
        out_shape=jax.ShapeDtypeStruct((WIDTH, tokens), bf16),
        in_specs=[pl.BlockSpec(memory_space=pl.ANY)] * 3,
        out_specs=pl.BlockSpec(memory_space=pltpu.VMEM),
        scratch_shapes=[
            pltpu.VMEM(queries.shape, bf16),
            pltpu.VMEM(keys.shape, bf16),
            pltpu.VMEM(values.shape, bf16),
            pltpu.VMEM((PAIRS, LANES, tokens), bf16),
            pltpu.VMEM((WIDTH, tokens), bf16),
            pltpu.VMEM((HEAD_COUNT, LANES, tokens), bf16),
            pltpu.VMEM((PAIRS, LANES, LANES), bf16),
            pltpu.VMEM((PAIRS, 1, LANES), jnp.float32),
            pltpu.VMEM((PAIRS, 1, LANES), jnp.float32),
            pltpu.VMEM((PAIRS, LANES, LANES), jnp.float32),
            pltpu.VMEM((2, chips[0], slots, 2 * WIDTH), bf16),
            pltpu.VMEM((2, chips[1], slots // 4, 2 * WIDTH), bf16),
            pltpu.VMEM((2, chips[2], 16, 2 * LANES), bf16),
            pltpu.SemaphoreType.DMA((3,)),
            pltpu.SemaphoreType.DMA((3,)),
            pltpu.SemaphoreType.DMA((3,)),
            pltpu.SemaphoreType.DMA((3,)),
            pltpu.SemaphoreType.DMA((3,)),
        ],
        compiler_params=pltpu.CompilerParams(
            collective_id=0, has_side_effects=True, vmem_limit_bytes=VMEM_LIMIT
        ),
        cost_estimate=pl.CostEstimate(
            flops=1_000_000_000, bytes_accessed=3_000_000, transcendentals=2_000_000
        ),
    )(queries, keys, values)
    return dot(combined, out_weight, ((0,), (0,))).astype(bf16)


def solution(mesh):
    in_specs = (P("seq", None), P("seq", None), P("seq", None), P())
    return jax.shard_map(
        on_device, mesh=mesh, in_specs=in_specs, out_specs=P("seq", None), check_vma=False
    )
```
